32 devices in a mesh: groups: 2 (over x), wide: 16 (over z, y, core).
Axes of the slice: x: 2, y: 2, z: 4, core: 2. Of those that a mesh axis runs over, the one named last changes fastest.
Arguments:
- tokens: bfloat16 [8192, 8192], P(('groups', 'wide')), parts along dimension 0, may hold values from -6 to 6
- cotangent: bfloat16 [8192, 1024], P(('groups', 'wide')), parts along dimension 0, may hold values from -6 to 6
- frozen_key_matrix: bfloat16 [8192, 1024], P('wide'), may hold values from -0.0625 to 0.0625
- adapter_down_weight: bfloat16 [64, 8192, 64], P(('groups', 'wide')), parts along dimension 0, may hold values from -0.0625 to 0.0625
- adapter_up_weight: bfloat16 [64, 64, 1024], P(('groups', 'wide')), parts along dimension 0, may hold values from -0.75 to 0.75
- token_adapter_index: int32 [8192, 1], P(('groups', 'wide')), parts along dimension 0, may hold values from 0 to 31; in each aligned block of 256 rows (0 to 255, 256 to 511, ...) at most 13 rows name the same one
- adapter_storage_index: int32 [64], P('groups'), parts along dimension 0, may hold values from 0 to 31, each once
Outputs:
- key_output: bfloat16 [8192, 1024], P(('groups', 'wide')), parts along dimension 0
- token_input_gradient: bfloat16 [8192, 8192], P(('groups', 'wide')), parts along dimension 0
- down_matrix_gradient: float32 [64, 8192, 64], P(('groups', 'wide')), parts along dimension 0
- up_matrix_gradient: float32 [64, 64, 1024], P(('groups', 'wide')), parts along dimension 0
The draws below stay inside these ranges and needn't reach their ends.
There are 2 independent parts, one for each index of `groups`. The reference program is written for one: setup_inputs(seed, part) draws one part's arguments, and reference() takes and returns one part's arrays. A program takes and returns all parts, laid end to end along the dimension named above; an argument that names none is the same for every part. Nothing has to cross between parts.
Inputs may be any that keep to these rules, and one draw needn't show every extreme that they name: `token_adapter_index`: among the rows of one device, each adapter is named by at most 13 rows. A permutation: the weights of adapter a stand at position adapter_storage_index[a] of adapter_down_weight and adapter_up_weight, on device adapter_storage_index[a] // 2 of wide.
All inputs are finite; a program needn't handle non-finite values.
Results may differ from the reference program's by a relative error of at most 0.0029.
Values may be sent and summed in bfloat16 or wider, within the bound.
No kernel may reach another device: no remote copies, remote signals or barrier semaphores. Data moves between devices by JAX's collectives and lax.ppermute only.
A program may use at most 128 MiB of HBM per device.

```python
import math
import jax
import jax.numpy as jnp
import numpy as np
from jax import lax

MODEL_WIDTH = 8192
KEY_FEATURES = 1024
ADAPTER_RANK = 64
TOK_DEV = 256
ADAPTER_TOTAL = 32
TOKENS = 4096
CAP_A = 13
N_WIDE = 16


def block_scale(key, shape, split, low, largest):
    loudness, own = 1.0, jax.random.fold_in(key, 6)
    for dim, shards_of in split:
        heights = jnp.exp(jax.random.uniform(jax.random.fold_in(own, dim), (shards_of,), jnp.float32, low / len(split), largest / len(split)))
        loudness = loudness * jnp.repeat(heights, shape[dim] // shards_of).reshape([-1 if axis == dim else 1 for axis in range(len(shape))])
    return loudness


def deal_out(own_key, own, number, rows, amount, top, bound, skew):
    ranking = jax.random.permutation(own_key, amount)
    packed, ordinary = shares(amount, rows * top, bound, skew, True), shares(amount, rows * top, bound, skew, False)
    places = jnp.arange(amount)

    def named(tallies, rotation):
        used = int((tallies > 0).sum())
        fixed = max(1, used // 4)
        moved = fixed + (places - fixed + rotation * (used - fixed)) % max(1, amount - fixed)
        return jnp.zeros((amount,), jnp.int32).at[ranking[jnp.where(places < fixed, places, moved)]].set(jnp.asarray(tallies, jnp.int32))

    tallies = jnp.where(number % 4 == 0, named(packed, number // 4), named(ordinary, number - number // 4 - 1))
    mixed = jax.random.permutation(jax.random.fold_in(own, 3), amount)
    giver, taker = mixed[0:amount // 2 * 2:2], mixed[1:amount // 2 * 2:2]
    slack = jnp.minimum(tallies[giver] - 1, bound - tallies[taker]) // 2
    slack = jnp.where((giver == ranking[0]) | (taker == ranking[0]) | (tallies[taker] == 0), 0, jnp.maximum(slack, 0))
    moved = jax.random.randint(jax.random.fold_in(own, 4), (amount // 2,), 0, 1 << 20) % (slack + 1)
    tallies = tallies.at[giver].add(-moved).at[taker].add(moved)
    items = jnp.searchsorted(jnp.cumsum(tallies), jnp.arange(rows * top), side="right").astype(jnp.int32)
    grid = items.reshape(top, rows).T
    grid = grid[jax.random.permutation(jax.random.fold_in(own, 1), rows)]
    rotation = jax.random.randint(jax.random.fold_in(own, 2), (rows, 1), 0, top)
    return jnp.take_along_axis(grid, (jnp.arange(top)[None, :] + rotation) % top, axis=1)


def shares(amount, total, limit, lean, full):
    portions = [(1 << 20) // math.isqrt(grade ** lean) + 1 for grade in range(1, amount + 1)]
    largest = limit if full else min(limit, max(-(-total // amount), total * portions[0] // sum(portions)))
    least = 1 if total - largest >= amount - 1 else 0
    given, surplus = [largest] + [least] * (amount - 1), total - largest - least * (amount - 1)
    while surplus > 0:
        movable = [i for i in range(1, amount) if given[i] < largest] or [i for i in range(1, amount) if given[i] < limit]
        whole, left = sum([portions[i] for i in movable]), surplus
        for i in movable:
            more = min(limit - given[i], max(1, left * portions[i] // whole), surplus)
            given[i] = given[i] + more
            surplus = surplus - more
    return np.array(given)


def scatter_about(key, dims, spread, most, split=(), kind=jnp.bfloat16):
    entries = jax.random.normal(key, dims, jnp.float32) * spread
    if len(split) > 0:
        entries = block_scale(key, dims, split, -0.22, 0.18) * entries
    return jnp.clip(entries, min=-most, max=most).astype(kind)


def setup_inputs(seed: int = 0, part: int = 0) -> dict:
    key_list = jax.random.split(jax.random.key(seed), 8)
    part_keys = jax.random.split(jax.random.fold_in(key_list[7], part), 8)
    tokens = scatter_about(part_keys[0], (TOKENS, MODEL_WIDTH), 1.0, 6.0, ((0, 16),))
    cotangent = scatter_about(part_keys[1], (TOKENS, KEY_FEATURES), 1.0, 6.0, ((0, 16),))
    frozen_key_matrix = scatter_about(key_list[2], (MODEL_WIDTH, KEY_FEATURES), MODEL_WIDTH ** -0.5, 0.0625, ((0, 16),))
    adapter_down_weight = scatter_about(part_keys[3], (ADAPTER_TOTAL, MODEL_WIDTH, ADAPTER_RANK), MODEL_WIDTH ** -0.5, 0.0625, ((0, 16),))
    adapter_up_weight = scatter_about(part_keys[4], (ADAPTER_TOTAL, ADAPTER_RANK, KEY_FEATURES), ADAPTER_RANK ** -0.5, 0.75, ((0, 16),))
    token_adapter_index_keys = jax.random.split(jax.random.fold_in(part_keys[5], 1), TOKENS // TOK_DEV)
    token_adapter_index_turns = jax.random.permutation(jax.random.fold_in(part_keys[5], 3), TOKENS // TOK_DEV)
    token_adapter_index = jax.vmap(lambda own, number: deal_out(jax.random.fold_in(part_keys[5], 2), own, number, TOK_DEV, ADAPTER_TOTAL, 1, CAP_A, 2))(token_adapter_index_keys, token_adapter_index_turns).reshape((TOKENS, 1))
    adapter_storage_index = jax.random.permutation(part_keys[6], ADAPTER_TOTAL).astype(jnp.int32)
    return dict(tokens=tokens, cotangent=cotangent, frozen_key_matrix=frozen_key_matrix, adapter_down_weight=adapter_down_weight, adapter_up_weight=adapter_up_weight, token_adapter_index=token_adapter_index, adapter_storage_index=adapter_storage_index)


adapter_scale = 0.25


def reference(tokens, cotangent, frozen_key_matrix, adapter_down_weight, adapter_up_weight, token_adapter_index, adapter_storage_index):
    flat_ids = token_adapter_index[:, 0].astype(jnp.int32)
    adapter_entries = adapter_storage_index.shape[0]
    most = N_WIDE * CAP_A
    onehot = (flat_ids[:, None] == jnp.arange(adapter_entries, dtype=jnp.int32)[None, :]).astype(jnp.int32)
    counts = jnp.sum(onehot, axis=0).astype(jnp.int32)
    starts = (jnp.cumsum(counts) - counts).astype(jnp.int32)
    order = jnp.argsort(flat_ids, stable=True).astype(jnp.int32)
    padded = jnp.concatenate([order, jnp.full((most,), TOKENS, jnp.int32)])

    def single_adapter(carry, adapter):
        out_acc, gradient_running_sum = carry
        picked = lax.dynamic_slice_in_dim(padded, starts[adapter].astype(jnp.int32), most)
        live = jnp.arange(most, dtype=jnp.int32) < counts[adapter]
        output_gradient = jnp.where(live, picked, TOKENS).astype(jnp.int32)
        safe = jnp.where(live, picked, 0).astype(jnp.int32)
        token_inputs = jnp.where(live[:, None], tokens[safe], jnp.zeros_like(tokens[safe]))
        gradient_tuple = jnp.where(live[:, None], cotangent[safe], jnp.zeros_like(cotangent[safe]))
        storage_position = adapter_storage_index[adapter]
        down_matrix = adapter_down_weight[storage_position]
        up_matrix = adapter_up_weight[storage_position]
        narrowed_rows = jnp.dot(token_inputs, down_matrix, preferred_element_type=jnp.float32).astype(jnp.bfloat16)
        widened_rows = (adapter_scale * jnp.dot(narrowed_rows, up_matrix, preferred_element_type=jnp.float32)).astype(jnp.bfloat16)
        hidden_gradient = jnp.dot(gradient_tuple, up_matrix.T, preferred_element_type=jnp.float32).astype(jnp.bfloat16)
        down_gradient_piece = adapter_scale * jnp.dot(token_inputs.T, hidden_gradient, preferred_element_type=jnp.float32)
        up_gradient_piece = adapter_scale * jnp.dot(narrowed_rows.T, gradient_tuple, preferred_element_type=jnp.float32)
        adapter_input = (adapter_scale * jnp.dot(hidden_gradient, down_matrix.T, preferred_element_type=jnp.float32)).astype(jnp.bfloat16)
        out_acc = out_acc.at[output_gradient].add(widened_rows.astype(jnp.float32), mode="drop")
        gradient_running_sum = gradient_running_sum.at[output_gradient].add(adapter_input.astype(jnp.float32), mode="drop")
        return (out_acc, gradient_running_sum), (down_gradient_piece, up_gradient_piece)

    initial_carry = (jnp.zeros((TOKENS, KEY_FEATURES), jnp.float32), jnp.zeros((TOKENS, MODEL_WIDTH), jnp.float32))
    (adapter_output, adapter_gradient), (down_matrices, up_matrices) = lax.scan(single_adapter, initial_carry, jnp.arange(adapter_entries, dtype=jnp.int32))
    frozen_path_output = jnp.dot(tokens, frozen_key_matrix, preferred_element_type=jnp.float32)
    frozen_path_gradient = jnp.dot(cotangent, frozen_key_matrix.T, preferred_element_type=jnp.float32)
    key_output = (frozen_path_output + adapter_output).astype(jnp.bfloat16)
    token_input_gradient = (frozen_path_gradient + adapter_gradient).astype(jnp.bfloat16)
    down_matrix_gradient = jnp.zeros_like(down_matrices).at[adapter_storage_index].set(down_matrices)
    up_matrix_gradient = jnp.zeros_like(up_matrices).at[adapter_storage_index].set(up_matrices)
    return key_output, token_input_gradient, down_matrix_gradient, up_matrix_gradient
```

```python
import jax
import jax.numpy as jnp
from jax import lax
from jax.sharding import PartitionSpec as P

adapter_scale = 0.25
bf16 = jnp.bfloat16
f32 = jnp.float32
CHAIN = 4


def dot(a, b, dims):
    return lax.dot_general(a, b, (dims, ((), ())), preferred_element_type=f32)


def shards(
    tokens,
    cotangent,
    frozen_key_matrix,
    adapter_down_weight,
    adapter_up_weight,
    token_adapter_index,
    adapter_storage_index,
):
    devices = lax.axis_size("wide")
    groups = lax.axis_size("groups")
    tok_count = tokens.shape[0]
    locals_, width, rank = adapter_down_weight.shape
    features = cotangent.shape[1]
    entries = adapter_storage_index.shape[0]
    capacity = max(2, 5 * tok_count // (3 * locals_ * devices))
    depth = CHAIN
    plane = devices // depth
    block = locals_ * rank
    me = lax.axis_index("wide")
    z, q = me // plane, me % plane
    group = lax.axis_index("groups")

    def shift(values, step, sources):
        pairs = [
            (s * plane + i, (s + step) * plane + i) for s in sources for i in range(plane)
        ]
        return lax.ppermute(values, "wide", pairs)

    def swap(values, mask):
        return lax.ppermute(values, "wide", [(i, i ^ mask) for i in range(devices)])

    def chain_gather(values):
        ups, downs = [], []
        up = down = values
        for k in range(1, depth):
            up = shift(up, 1, range(k - 1, depth - 1))
            down = shift(down, -1, range(1, depth - k + 1))
            ups.append(up)
            downs.append(down)
        line = jnp.concatenate(ups[::-1] + [values] + downs, axis=0)
        rows = values.shape[0]
        return lax.dynamic_slice_in_dim(line, (depth - 1 - z) * rows, depth * rows, 0)

    def chain_reduce(parts, own):
        up = down = None
        for k in range(1, depth):
            far = depth - k
            here_up = lax.dynamic_index_in_dim(parts, jnp.minimum(z + far, depth - 1), 0, False)
            here_down = lax.dynamic_index_in_dim(parts, jnp.maximum(z - far, 0), 0, False)
            if up is not None:
                here_up = (here_up.astype(f32) + up.astype(f32)).astype(bf16)
                here_down = (here_down.astype(f32) + down.astype(f32)).astype(bf16)
            up = shift(here_up, 1, range(0, k))
            down = shift(here_down, -1, range(depth - k, depth))
        return own + up.astype(f32) + down.astype(f32)

    share = frozen_key_matrix.shape[0] // groups
    down_rows = jnp.transpose(adapter_down_weight, (0, 2, 1)).reshape(block, width)
    up_rows = adapter_up_weight.reshape(block, features)

    flat_ids = token_adapter_index[:, 0]
    onehot = (flat_ids[:, None] == jnp.arange(entries, dtype=jnp.int32)[None, :]).astype(jnp.int32)
    within = jnp.sum(jnp.cumsum(onehot, axis=0) * onehot, axis=1) - 1
    position = jnp.sum(onehot * adapter_storage_index[None, :], axis=1)
    home, local = position // locals_, position % locals_
    relative = (home % plane) ^ q
    rows = depth * locals_ * capacity
    slots = ((relative * depth + home // plane) * locals_ + local) * capacity + within
    spread = (
        jnp.arange(plane * rows, dtype=jnp.int32)[:, None] == slots[None, :]
    ).astype(bf16)

    def dispatch(values):
        out = []
        for m in range(plane):
            part = dot(spread[m * rows : (m + 1) * rows], values, ((1,), (0,))).astype(bf16)
            out.append(part if m == 0 else swap(part, m))
        return jnp.concatenate(out, axis=0)

    def give_back(values):
        out = []
        for m in range(plane):
            part = values[m * rows : (m + 1) * rows]
            out.append(part if m == 0 else swap(part, m))
        return jnp.concatenate(out, axis=0)

    up_all = chain_gather(up_rows)
    down_all = chain_gather(down_rows)
    cot = dispatch(cotangent)
    token_inputs = dispatch(tokens)

    row_adapter = (jnp.arange(plane * rows) % rows) // capacity
    col_adapter = jnp.arange(depth * block) // rank
    mask = row_adapter[:, None] == col_adapter[None, :]

    def masked(values):
        return jnp.where(mask, values, 0.0).astype(bf16)

    hidden = masked(dot(cot, up_all, ((1,), (1,))))
    own_cols = lambda v: lax.dynamic_slice_in_dim(v, z * block, block, 1)
    down_parts = (adapter_scale * dot(hidden, token_inputs, ((0,), (0,)))).astype(bf16)
    down_own = adapter_scale * dot(own_cols(hidden), token_inputs, ((0,), (0,)))
    down_grad = chain_reduce(down_parts.reshape(depth, block, width), down_own)

    lora_input = (adapter_scale * dot(hidden, down_all, ((1,), (0,)))).astype(bf16)
    lora_back = give_back(lora_input)

    shrunk = masked(dot(token_inputs, down_all, ((1,), (1,))))
    expanded = (adapter_scale * dot(shrunk, up_all, ((1,), (0,)))).astype(bf16)
    expanded_back = give_back(expanded)
    up_parts = (adapter_scale * dot(shrunk, cot, ((0,), (0,)))).astype(bf16)
    up_own = adapter_scale * dot(own_cols(shrunk), cot, ((0,), (0,)))
    up_grad = chain_reduce(up_parts.reshape(depth, block, features), up_own)

    piece = lax.dynamic_slice_in_dim(frozen_key_matrix, group * share, share, 0)
    gathered = chain_gather(piece).reshape(depth, 1, 1, share, features)

    def join(values, mask):
        other = swap(values, mask)
        low = (q & mask) == 0
        return jnp.where(
            low, jnp.concatenate([values, other], 1), jnp.concatenate([other, values], 1)
        )

    bit = 2
    while bit < plane:
        gathered = join(gathered, bit)
        bit *= 2
    sides = [gathered] + [
        lax.ppermute(gathered, "groups", [(i, (i + s) % groups) for i in range(groups)])
        for s in range(1, groups)
    ]
    sides = jnp.concatenate(sides[::-1] + sides[:0:-1], 2)
    gathered = lax.dynamic_slice_in_dim(sides, groups - 1 - group, groups, 2)
    mate = swap(gathered, 1)
    even = jnp.where(q % 2 == 0, gathered, mate)
    odd = jnp.where(q % 2 == 0, mate, gathered)
    whole = jnp.stack([even, odd], 2).reshape(width, features)

    frozen_out = dot(tokens, whole, ((1,), (0,)))
    frozen_grad = dot(cotangent, whole, ((1,), (1,)))
    key_output = (frozen_out + dot(spread, expanded_back, ((0,), (0,)))).astype(bf16)
    token_grad = (frozen_grad + dot(spread, lora_back, ((0,), (0,)))).astype(bf16)
    down_grad = jnp.transpose(down_grad.reshape(locals_, rank, width), (0, 2, 1))
    up_grad = up_grad.reshape(locals_, rank, features)
    return key_output, token_grad, down_grad, up_grad


def solution(mesh):
    return jax.shard_map(
        shards,
        mesh=mesh,
        in_specs=(
            P(("groups", "wide"), None),
            P(("groups", "wide"), None),
            P("wide", None),
            P(("groups", "wide"), None, None),
            P(("groups", "wide"), None, None),
            P(("groups", "wide"), None),
            P("groups"),
        ),
        out_specs=(
            P(("groups", "wide"), None),
            P(("groups", "wide"), None),
            P(("groups", "wide"), None, None),
            P(("groups", "wide"), None, None),
        ),
        check_vma=False,
    )
```

```python
import jax
import jax.numpy as jnp
from jax import lax
from jax.sharding import PartitionSpec as P

adapter_scale = 0.25
bf16 = jnp.bfloat16
f32 = jnp.float32
CHAIN = 4
ORDER = ((3, 2, 1, 0), (3, 2, 0, 1), (0, 1, 3, 2), (0, 1, 2, 3))
RANK = tuple(tuple(row.index(k) for k in range(CHAIN)) for row in ORDER)


def dot(a, b, dims):
    return lax.dot_general(a, b, (dims, ((), ())), preferred_element_type=f32)


def gate(values, after):
    return lax.optimization_barrier((values, after))[0]


def shards(
    tokens,
    cotangent,
    frozen_key_matrix,
    adapter_down_weight,
    adapter_up_weight,
    token_adapter_index,
    adapter_storage_index,
):
    devices = lax.axis_size("wide")
    groups = lax.axis_size("groups")
    tok_count = tokens.shape[0]
    locals_, width, rank = adapter_down_weight.shape
    features = cotangent.shape[1]
    entries = adapter_storage_index.shape[0]
    capacity = max(2, 5 * tok_count // (3 * locals_ * devices))
    depth = CHAIN
    plane = devices // depth
    block = locals_ * rank
    half = width // 2
    rows = depth * locals_ * capacity
    me = lax.axis_index("wide")
    z, q = me // plane, me % plane
    group = lax.axis_index("groups")
    edge = (z == 0) | (z == depth - 1)
    order = lax.dynamic_index_in_dim(jnp.array(ORDER, jnp.int32), z, 0, False)
    place = lax.dynamic_index_in_dim(jnp.array(RANK, jnp.int32), z, 0, False)

    def along(values, moves):
        pairs = [(s * plane + i, d * plane + i) for s, d in moves for i in range(plane)]
        return lax.ppermute(values, "wide", pairs)

    def swap(values, mask):
        return lax.ppermute(values, "wide", [(i, i ^ mask) for i in range(devices)])

    def turn(values, k):
        return along(values, [(i, (i + k) % depth) for i in range(depth)])

    UP = [(0, 1), (1, 2), (2, 3)]
    DOWN = [(1, 0), (2, 1), (3, 2)]

    def gather1(v):
        return along(v, UP), along(v, DOWN)

    def gather2(u1, d1):
        return along(u1, UP[1:]), along(d1, DOWN[:2])

    def pick2(uu, dd):
        return jnp.where(z >= 2, uu, dd)

    def gather3(e2):
        return along(e2, [(2, 3), (1, 0)])

    def chunk1(u1, d1, e2):
        return jnp.where(edge, e2, jnp.where(z == 1, d1, u1))

    def chunk2(u1, d1):
        return jnp.where((z == 0) | (z == 2), d1, u1)

    down_rows = jnp.transpose(adapter_down_weight, (0, 2, 1)).reshape(block, width)
    up_rows = adapter_up_weight.reshape(block, features)
    share = frozen_key_matrix.shape[0] // groups
    piece = lax.dynamic_slice_in_dim(frozen_key_matrix, group * share, share, 0)

    flat_ids = token_adapter_index[:, 0]
    onehot = (flat_ids[:, None] == jnp.arange(entries, dtype=jnp.int32)[None, :]).astype(jnp.int32)
    within = jnp.sum(jnp.cumsum(onehot, axis=0) * onehot, axis=1) - 1
    position = jnp.sum(onehot * adapter_storage_index[None, :], axis=1)
    home, local = position // locals_, position % locals_
    far = home // plane
    chunk = jnp.sum(
        jnp.where(far[:, None] == jnp.arange(depth, dtype=jnp.int32)[None, :], place[None, :], 0),
        axis=1,
    )
    relative = (home % plane) ^ q
    slots = ((relative * depth + chunk) * locals_ + local) * capacity + within
    spread = (
        jnp.arange(plane * rows, dtype=jnp.int32)[:, None] == slots[None, :]
    ).astype(bf16)

    def part(values, m):
        return dot(spread[m * rows : (m + 1) * rows], values, ((1,), (0,))).astype(bf16)

    def dispatch(values):
        return [part(values, 0)] + [swap(part(values, m), m) for m in range(1, plane)]

    def give_back(values):
        split = [values[m * rows : (m + 1) * rows] for m in range(plane)]
        return split[:1] + [swap(split[m], m) for m in range(1, plane)]

    def join_plane(values):
        values = values.reshape(1, 1, 1, *values.shape)
        bit = 2
        while bit < plane:
            other = swap(values, bit)
            low = (q & bit) == 0
            values = jnp.where(
                low, jnp.concatenate([values, other], 0), jnp.concatenate([other, values], 0)
            )
            bit *= 2
        return values

    def join_groups(values):
        sides = [values] + [
            lax.ppermute(values, "groups", [(i, (i + s) % groups) for i in range(groups)])
            for s in range(1, groups)
        ]
        sides = jnp.concatenate(sides[::-1] + sides[:0:-1], 2)
        return lax.dynamic_slice_in_dim(sides, groups - 1 - group, groups, 2)

    def join_cores(values):
        mate = swap(values, 1)
        first = q % 2 == 0
        both = jnp.concatenate(
            [jnp.where(first, values, mate), jnp.where(first, mate, values)], 1
        )
        return both.reshape(width // depth, features)

    row_adapter = (jnp.arange(plane * rows) % rows) // capacity
    col_adapter = jnp.arange(depth * block) // rank
    mask = row_adapter[:, None] == col_adapter[None, :]

    def masked(values):
        return jnp.where(mask, values, 0.0).astype(bf16)

    def grad(hid, values, extra=()):
        out = adapter_scale * dot(hid, values, ((0,), (0,)))
        for more in extra:
            out = out + more.astype(f32)
        return out

    a0, a1 = down_rows[:, :half], down_rows[:, half:]
    u1_0, d1_0 = gather1(a0)
    turned = [turn(up_rows, k) for k in range(1, depth)]
    cots = dispatch(cotangent)
    x0s = dispatch(tokens[:, :half])

    a1, t1, piece = gate((a1, tokens[:, half:], piece), (cots, turned))
    u1_1, d1_1 = gather1(a1)
    x1s = dispatch(t1)
    wu1, wd1 = gather1(piece)
    y3 = join_plane(piece)

    by_shift = jnp.stack([up_rows] + turned)
    up_all = jnp.concatenate(
        [
            lax.dynamic_index_in_dim(by_shift, (z - order[j] + depth) % depth, 0, False)
            for j in range(depth)
        ],
        axis=0,
    )
    cot = jnp.concatenate(cots, axis=0)
    hidden = masked(dot(cot, up_all, ((1,), (1,))))
    h0, h1, h2, h3 = (hidden[:, j * block : (j + 1) * block] for j in range(depth))
    second = jnp.where(edge, h1, h0)
    third_up = jnp.where(z == 1, h1, h2)
    third_down = jnp.where(z == 2, h1, h2)

    def reduce1(x):
        return along(grad(h0, x).astype(bf16), [(0, 1), (3, 2)])

    def reduce2(x, r1):
        v = grad(second, x, (r1,)).astype(bf16)
        return along(v, UP[:2]), along(v, DOWN[1:])

    def reduce3(x, ru, rd):
        return (
            along(grad(third_up, x, (ru,)).astype(bf16), UP),
            along(grad(third_down, x, (rd,)).astype(bf16), DOWN),
        )

    x0 = jnp.concatenate(x0s, axis=0)
    uu_0, dd_0 = gather2(u1_0, d1_0)
    r1_0 = reduce1(x0)
    w2 = chunk2(wu1, wd1)
    wuu, wdd = gather2(wu1, wd1)
    y2 = join_plane(w2)
    g3 = join_groups(y3)

    x1 = jnp.concatenate(x1s, axis=0)
    u1_1, d1_1 = gate((u1_1, d1_1), (u1_0, d1_0, x0s))
    uu_1, dd_1 = gather2(u1_1, d1_1)
    r1_1 = reduce1(x1)
    we2 = pick2(wuu, wdd)
    w1 = chunk1(wu1, wd1, we2)
    we3 = gather3(we2)
    y1 = join_plane(w1)
    g2 = join_groups(y2)

    e2_0 = pick2(uu_0, dd_0)
    e3_0 = gather3(e2_0)
    r2u_0, r2d_0 = reduce2(x0, r1_0)
    w0 = jnp.where(edge, we3, we2)
    y0 = join_plane(w0)
    g1 = join_groups(y1)
    f3 = join_cores(g3)
    f2 = join_cores(g2)

    e2_1 = pick2(uu_1, dd_1)
    e3_1 = gather3(e2_1)
    r2u_1, r2d_1 = reduce2(x1, r1_1)
    down_0 = jnp.concatenate(
        [jnp.where(edge, e3_0, e2_0), chunk1(u1_0, d1_0, e2_0), chunk2(u1_0, d1_0), a0], axis=0
    )
    lora_0 = (adapter_scale * dot(hidden, down_0, ((1,), (0,)))).astype(bf16)
    back_0 = give_back(lora_0)
    g0 = join_groups(y0)
    f1 = join_cores(g1)

    r3u_0, r3d_0 = reduce3(x0, r2u_0, r2d_0)
    down_1 = jnp.concatenate(
        [jnp.where(edge, e3_1, e2_1), chunk1(u1_1, d1_1, e2_1), chunk2(u1_1, d1_1), a1], axis=0
    )
    lora_1 = (adapter_scale * dot(hidden, down_1, ((1,), (0,)))).astype(bf16)
    back_1 = give_back(lora_1)
    shrunk = masked(dot(x0, down_0, ((1,), (1,))) + dot(x1, down_1, ((1,), (1,))))
    up_own = adapter_scale * dot(shrunk[:, 3 * block :], cot, ((0,), (0,)))
    up_parts = (adapter_scale * dot(shrunk, cot, ((0,), (0,)))).astype(bf16)
    up_parts = up_parts.reshape(depth, block, features)
    up_sent = [
        turn(
            lax.dynamic_index_in_dim(up_parts, place[(z + k) % depth], 0, False),
            k,
        )
        for k in range(1, depth)
    ]
    expanded = (adapter_scale * dot(shrunk, up_all, ((1,), (0,)))).astype(bf16)
    expanded_back = give_back(expanded)
    f0 = join_cores(g0)

    r3u_1, r3d_1 = reduce3(x1, r2u_1, r2d_1)
    whole = jnp.zeros((depth, width // depth, features), bf16)
    for j, f in enumerate((f0, f1, f2, f3)):
        whole = lax.dynamic_update_slice_in_dim(whole, f[None], order[j], 0)
    whole = whole.reshape(width, features)
    key_output = (
        dot(tokens, whole, ((1,), (0,)))
        + dot(spread, jnp.concatenate(expanded_back, 0), ((0,), (0,)))
    ).astype(bf16)
    token_grad = jnp.concatenate(
        [
            (
                dot(cotangent, whole[h * half : (h + 1) * half], ((1,), (1,)))
                + dot(spread, jnp.concatenate(back, 0), ((0,), (0,)))
            ).astype(bf16)
            for h, back in ((0, back_0), (1, back_1))
        ],
        axis=1,
    )
    down_grad = jnp.concatenate(
        [grad(h3, x0, (r3u_0, r3d_0)), grad(h3, x1, (r3u_1, r3d_1))], axis=1
    )
    up_grad = up_own + sum(v.astype(f32) for v in up_sent)
    down_grad = jnp.transpose(down_grad.reshape(locals_, rank, width), (0, 2, 1))
    up_grad = up_grad.reshape(locals_, rank, features)
    return key_output, token_grad, down_grad, up_grad


def solution(mesh):
    return jax.shard_map(
        shards,
        mesh=mesh,
        in_specs=(
            P(("groups", "wide"), None),
            P(("groups", "wide"), None),
            P("wide", None),
            P(("groups", "wide"), None, None),
            P(("groups", "wide"), None, None),
            P(("groups", "wide"), None),
            P("groups"),
        ),
        out_specs=(
            P(("groups", "wide"), None),
            P(("groups", "wide"), None),
            P(("groups", "wide"), None, None),
            P(("groups", "wide"), None, None),
        ),
        check_vma=False,
    )
```

```python
import jax
import jax.numpy as jnp
from jax import lax
from jax.sharding import Mesh, PartitionSpec as P

adapter_scale = 0.25
bf16 = jnp.bfloat16
f32 = jnp.float32
CHAIN = 4
ORDER = ((3, 2, 1, 0), (3, 2, 0, 1), (0, 1, 3, 2), (0, 1, 2, 3))
RANK = tuple(tuple(row.index(k) for k in range(CHAIN)) for row in ORDER)


def dot(a, b, dims):
    return lax.dot_general(a, b, (dims, ((), ())), preferred_element_type=f32)


def gate(values, after):
    return lax.optimization_barrier((values, after))[0]


def shards(
    tokens,
    cotangent,
    frozen_key_matrix,
    adapter_down_weight,
    adapter_up_weight,
    token_adapter_index,
    adapter_storage_index,
):
    groups = lax.axis_size("groups")
    depth = lax.axis_size("chain")
    sides = lax.axis_size("side")
    plane = 2 * sides
    devices = depth * plane
    tok_count = tokens.shape[0]
    locals_, width, rank = adapter_down_weight.shape
    features = cotangent.shape[1]
    entries = adapter_storage_index.shape[0]
    capacity = max(2, 5 * tok_count // (3 * locals_ * devices))
    block = locals_ * rank
    half = width // 2
    rows = depth * locals_ * capacity
    z = lax.axis_index("chain")
    side = lax.axis_index("side")
    q = 2 * side + lax.axis_index("core")
    group = lax.axis_index("groups")
    edge = (z == 0) | (z == depth - 1)
    order = lax.dynamic_index_in_dim(jnp.array(ORDER, jnp.int32), z, 0, False)
    place = lax.dynamic_index_in_dim(jnp.array(RANK, jnp.int32), z, 0, False)

    def swap(values, bit):
        if bit == 1:
            return lax.ppermute(values, "core", [(0, 1), (1, 0)])
        return lax.ppermute(values, "side", [(i, i ^ (bit // 2)) for i in range(sides)])

    def turn(values, k):
        return lax.ppermute(values, "chain", [(i, (i + k) % depth) for i in range(depth)])

    def up(values):
        return lax.ppermute(values, "chain", [(i, i + 1) for i in range(depth - 1)])

    def down(values):
        return lax.ppermute(values, "chain", [(i + 1, i) for i in range(depth - 1)])

    bits = []
    while 2 ** len(bits) < plane:
        bits.append(2 ** len(bits))

    down_rows = jnp.transpose(adapter_down_weight, (0, 2, 1)).reshape(block, width)
    up_rows = adapter_up_weight.reshape(block, features)
    share = frozen_key_matrix.shape[0] // groups
    piece = lax.dynamic_slice_in_dim(frozen_key_matrix, group * share, share, 0)
    extra = share * features // block

    def pack(values):
        if share >= block:
            return jnp.concatenate([values[i : i + block] for i in range(0, share, block)], 1)
        return jnp.concatenate([values[:, i : i + extra] for i in range(0, features, extra)], 0)

    def unpack(values):
        if share >= block:
            return jnp.concatenate(
                [values[:, i : i + features] for i in range(0, extra, features)], 0
            )
        return jnp.concatenate([values[i : i + share] for i in range(0, block, share)], 1)

    flat_ids = token_adapter_index[:, 0]
    onehot = (flat_ids[:, None] == jnp.arange(entries, dtype=jnp.int32)[None, :]).astype(jnp.int32)
    within = jnp.sum(jnp.cumsum(onehot, axis=0) * onehot, axis=1) - 1
    position = jnp.sum(onehot * adapter_storage_index[None, :], axis=1)
    home, local = position // locals_, position % locals_
    far = home // plane
    chunk = jnp.sum(
        jnp.where(far[:, None] == jnp.arange(depth, dtype=jnp.int32)[None, :], place[None, :], 0),
        axis=1,
    )
    relative = (home % plane) ^ q
    slots = ((relative * depth + chunk) * locals_ + local) * capacity + within
    spread = (
        jnp.arange(plane * rows, dtype=jnp.int32)[:, None] == slots[None, :]
    ).astype(bf16)

    def dispatch(values):
        cut = spread.reshape(plane // 2, 2, rows, tok_count)
        first = [
            dot(cut[:, i].reshape(plane // 2 * rows, tok_count), values, ((1,), (0,))).astype(bf16)
            for i in range(2)
        ]
        sent = swap(first[1], 1)
        parts = [
            jnp.concatenate([v[m * rows : (m + 1) * rows] for v in (first[0], sent)], 0)
            for m in range(plane // 2)
        ]
        for bit in bits[1:]:
            got = swap(jnp.concatenate(parts[1::2], 0), bit)
            size = parts[0].shape[0]
            parts = [
                jnp.concatenate([v, got[i * size : (i + 1) * size]], 0)
                for i, v in enumerate(parts[::2])
            ]
        return parts[0]

    def give_back(values):
        parts = [values]
        for bit in bits[::-1]:
            size = parts[0].shape[0] // 2
            got = swap(jnp.concatenate([v[size:] for v in parts], 0), bit)
            parts = [v[:size] for v in parts] + [
                got[i * size : (i + 1) * size] for i in range(len(parts))
            ]
        index = [0]
        for bit in bits[::-1]:
            index = index + [m | bit for m in index]
        return jnp.concatenate([parts[index.index(m)] for m in range(plane)], 0)

    def join_sides(values):
        values = values[:, None]
        for bit in bits[1:]:
            other = swap(values, bit)
            low = (q & bit) == 0
            values = jnp.concatenate(
                [jnp.where(low, values, other), jnp.where(low, other, values)], 1
            )
        return values

    def join_rest(values):
        everything = lax.all_gather(values, ("groups", "core"), axis=0, tiled=False)
        everything = everything.reshape(groups, 2, *values.shape)
        everything = jnp.transpose(everything, (2, 3, 1, 0, 4, 5))
        return everything.reshape(values.shape[0], width // depth, features)

    row_adapter = (jnp.arange(plane * rows) % rows) // capacity
    col_adapter = jnp.arange(depth * block) // rank
    mask = row_adapter[:, None] == col_adapter[None, :]

    def masked(values):
        return jnp.where(mask, values, 0.0).astype(bf16)

    def grad(hid, values, *more):
        out = adapter_scale * dot(hid, values, ((0,), (0,)))
        for m in more:
            out = out + m.astype(f32)
        return out

    def widen(values, like):
        return jnp.pad(values, ((0, 0), (0, like.shape[1] - values.shape[1])))

    def near(u1, d1):
        return jnp.where((z == 0) | (z == 2), d1, u1)

    def middle(u1, d1, e2):
        return jnp.where(edge, e2, jnp.where(z == 1, d1, u1))

    turned = [turn(up_rows, k) for k in range(1, depth)]
    cot = dispatch(cotangent)

    a = [down_rows[:, :half], down_rows[:, half:]]
    tok = [tokens[:, :half], tokens[:, half:]]
    load = [jnp.concatenate([a[0], pack(piece)], 1), a[1]]
    load[0] = gate(load[0], turned)
    one, x = [None, None], [None, None]
    for h in range(2):
        one[h] = up(load[h]), down(load[h])
        x[h] = dispatch(gate(tok[h], cot) if h == 0 else gate(tok[h], x[0]))

    by_shift = jnp.stack([up_rows] + turned)
    up_all = jnp.concatenate(
        [
            lax.dynamic_index_in_dim(by_shift, (z - order[j] + depth) % depth, 0, False)
            for j in range(depth)
        ],
        axis=0,
    )
    hidden = masked(dot(cot, up_all, ((1,), (1,))))
    hid = [hidden[:, j * block : (j + 1) * block] for j in range(depth)]
    second = jnp.where(edge, hid[1], hid[0])
    third_up = jnp.where(z == 1, hid[1], hid[2])
    third_down = jnp.where(z == 2, hid[1], hid[2])

    def pair(p):
        cut = hidden.reshape(plane, 2, rows // 2, depth * block)[:, p]
        return cut.reshape(plane * rows // 2, depth * block)[
            :, p * 2 * block : (p + 1) * 2 * block
        ]

    def spread_pair(p):
        return spread.reshape(plane, 2, rows // 2, tok_count)[:, p].reshape(-1, tok_count)

    def lora(p, weights):
        return (adapter_scale * dot(pair(p), weights, ((1,), (0,)))).astype(bf16)

    def weight_part(values):
        return values[:, :half]

    def base_part(values):
        return unpack(values[:, half:])

    two = [None, None]
    for h in range(2):
        v = widen(grad(hid[0], x[h]).astype(bf16), load[h])
        two[h] = (
            up(jnp.where(z == 0, v, one[h][0])),
            down(jnp.where(z == depth - 1, v, one[h][1])),
        )
    base_32 = join_rest(join_sides(jnp.stack([base_part(near(*one[0])), piece])))
    near_a = jnp.concatenate([near(*map(weight_part, one[h])) for h in range(2)], 1)
    back_1 = give_back(lora(1, jnp.concatenate([near_a, down_rows], 0)))

    three, e2 = [None, None], [None, None]
    for h in range(2):
        uu, dd = two[h]
        e2[h] = jnp.where(z >= 2, uu, dd)
        r1 = jnp.where(edge, jnp.zeros_like(uu), jnp.where(z == 1, uu, dd))
        v = widen(grad(second, x[h], weight_part(r1)).astype(bf16), load[h])
        three[h] = up(jnp.where(z <= 1, v, e2[h])), down(jnp.where(z >= 2, v, e2[h]))
    base_1 = join_rest(join_sides(base_part(middle(*one[0], e2[0]))[None]))

    four, far_a, back_0 = [None, None], [None, None], [None, None]
    for h in range(2):
        uu, dd = map(weight_part, three[h])
        e3 = jnp.where(z == depth - 1, uu, dd)
        zero = jnp.zeros_like(uu)
        ru, rd = jnp.where(edge, zero, uu), jnp.where(edge, zero, dd)
        four[h] = (
            up(grad(third_up, x[h], ru).astype(bf16)),
            down(grad(third_down, x[h], rd).astype(bf16)),
        )
        far_a[h] = jnp.concatenate(
            [
                jnp.where(edge, e3, weight_part(e2[h])),
                middle(*map(weight_part, one[h]), weight_part(e2[h])),
            ],
            0,
        )
        back_0[h] = give_back(lora(0, far_a[h]))
    uu, dd = three[0]
    base_0 = join_rest(
        join_sides(
            base_part(jnp.where(edge, jnp.where(z == depth - 1, uu, dd), e2[0]))[None]
        )
    )

    down_all = jnp.concatenate([jnp.concatenate(far_a, 1), near_a, down_rows], 0)
    shrunk = masked(
        sum(
            dot(x[h], down_all[:, h * half : (h + 1) * half], ((1,), (1,))) for h in range(2)
        )
    )
    up_parts = adapter_scale * dot(shrunk, cot, ((0,), (0,)))
    up_own = up_parts[(depth - 1) * block :]
    up_parts = up_parts.astype(bf16).reshape(depth, block, features)
    up_sent = [
        turn(lax.dynamic_index_in_dim(up_parts, place[(z + k) % depth], 0, False), k)
        for k in range(1, depth)
    ]
    expanded = give_back((adapter_scale * dot(shrunk, up_all, ((1,), (0,)))).astype(bf16))

    whole = jnp.zeros((depth, width // depth, features), bf16)
    for j, f in ((3, base_32[1:]), (2, base_32[:1]), (1, base_1), (0, base_0)):
        whole = lax.dynamic_update_slice_in_dim(whole, f, order[j], 0)
    whole = whole.reshape(width, features)
    key_output = (
        dot(tokens, whole, ((1,), (0,))) + dot(spread, expanded, ((0,), (0,)))
    ).astype(bf16)
    token_grad = (
        dot(cotangent, whole, ((1,), (1,)))
        + dot(spread_pair(1), back_1, ((0,), (0,)))
        + dot(spread_pair(0), jnp.concatenate(back_0, 1), ((0,), (0,)))
    ).astype(bf16)
    down_grad = jnp.concatenate([grad(hid[3], x[h], *four[h]) for h in range(2)], axis=1)
    up_grad = up_own + sum(v.astype(f32) for v in up_sent)
    down_grad = jnp.transpose(down_grad.reshape(locals_, rank, width), (0, 2, 1))
    up_grad = up_grad.reshape(locals_, rank, features)
    return key_output, token_grad, down_grad, up_grad


def solution(mesh):
    groups, wide = mesh.devices.shape
    fine = Mesh(
        mesh.devices.reshape(groups, CHAIN, wide // CHAIN // 2, 2),
        ("groups", "chain", "side", "core"),
    )
    every = ("groups", "chain", "side", "core")
    return jax.shard_map(
        shards,
        mesh=fine,
        in_specs=(
            P(every, None),
            P(every, None),
            P(every[1:], None),
            P(every, None, None),
            P(every, None, None),
            P(every, None),
            P("groups"),
        ),
        out_specs=(
            P(every, None),
            P(every, None),
            P(every, None, None),
            P(every, None, None),
        ),
        check_vma=False,
    )
```

```python
import jax
import jax.numpy as jnp
from jax import lax
from jax.experimental import pallas as pl
from jax.sharding import Mesh, PartitionSpec as P

adapter_scale = 0.25
bf16 = jnp.bfloat16
f32 = jnp.float32
CHAIN = 4
ORDER = ((3, 2, 1, 0), (3, 2, 0, 1), (0, 1, 3, 2), (0, 1, 2, 3))
RANK = tuple(tuple(row.index(k) for k in range(CHAIN)) for row in ORDER)


def dot(a, b, dims):
    return lax.dot_general(a, b, (dims, ((), ())), preferred_element_type=f32)


def tie(value, *after):
    def body(*refs):
        pass

    anywhere = pl.BlockSpec(memory_space=pl.ANY)
    return pl.pallas_call(
        body,
        out_shape=jax.ShapeDtypeStruct(value.shape, value.dtype),
        in_specs=[anywhere] * (1 + len(after)),
        out_specs=anywhere,
        input_output_aliases={0: 0},
        cost_estimate=pl.CostEstimate(flops=0, bytes_accessed=0, transcendentals=0),
    )(value, *after)


def shards(
    tokens,
    cotangent,
    frozen_key_matrix,
    adapter_down_weight,
    adapter_up_weight,
    token_adapter_index,
    adapter_storage_index,
):
    groups = lax.axis_size("groups")
    depth = lax.axis_size("chain")
    sides = lax.axis_size("side")
    plane = 2 * sides
    devices = depth * plane
    tok_count = tokens.shape[0]
    locals_, width, rank = adapter_down_weight.shape
    features = cotangent.shape[1]
    entries = adapter_storage_index.shape[0]
    capacity = max(2, 5 * tok_count // (3 * locals_ * devices))
    block = locals_ * rank
    half = width // 2
    rows = depth * locals_ * capacity
    z = lax.axis_index("chain")
    side = lax.axis_index("side")
    q = 2 * side + lax.axis_index("core")
    group = lax.axis_index("groups")
    edge = (z == 0) | (z == depth - 1)
    order = lax.dynamic_index_in_dim(jnp.array(ORDER, jnp.int32), z, 0, False)
    place = lax.dynamic_index_in_dim(jnp.array(RANK, jnp.int32), z, 0, False)

    def swap(values, bit):
        if bit == 1:
            return lax.ppermute(values, "core", [(0, 1), (1, 0)])
        return lax.ppermute(values, "side", [(i, i ^ (bit // 2)) for i in range(sides)])

    def turn(values, k):
        return lax.ppermute(values, "chain", [(i, (i + k) % depth) for i in range(depth)])

    def up(values):
        return lax.ppermute(values, "chain", [(i, i + 1) for i in range(depth - 1)])

    def down(values):
        return lax.ppermute(values, "chain", [(i + 1, i) for i in range(depth - 1)])

    bits = []
    while 2 ** len(bits) < plane:
        bits.append(2 ** len(bits))

    down_rows = jnp.transpose(adapter_down_weight, (0, 2, 1)).reshape(block, width)
    up_rows = adapter_up_weight.reshape(block, features)
    share = frozen_key_matrix.shape[0] // groups
    piece = lax.dynamic_slice_in_dim(frozen_key_matrix, group * share, share, 0)
    flat_ids = token_adapter_index[:, 0]
    onehot = (flat_ids[:, None] == jnp.arange(entries, dtype=jnp.int32)[None, :]).astype(jnp.int32)
    within = jnp.sum(jnp.cumsum(onehot, axis=0) * onehot, axis=1) - 1
    position = jnp.sum(onehot * adapter_storage_index[None, :], axis=1)
    home, local = position // locals_, position % locals_
    far = home // plane
    chunk = jnp.sum(
        jnp.where(far[:, None] == jnp.arange(depth, dtype=jnp.int32)[None, :], place[None, :], 0),
        axis=1,
    )
    relative = (home % plane) ^ q
    slots = ((relative * depth + chunk) * locals_ + local) * capacity + within
    spread = (
        jnp.arange(plane * rows, dtype=jnp.int32)[:, None] == slots[None, :]
    ).astype(bf16)

    def dispatch(spread, values, *after):
        rows = spread.shape[0] // plane
        cut = spread.reshape(plane // 2, 2, rows, tok_count)
        first = [
            dot(cut[:, i].reshape(plane // 2 * rows, tok_count), values, ((1,), (0,))).astype(bf16)
            for i in range(2)
        ]
        if after:
            first[1] = tie(first[1], *after)
        sent = swap(first[1], 1)
        parts = [
            jnp.concatenate([v[m * rows : (m + 1) * rows] for v in (first[0], sent)], 0)
            for m in range(plane // 2)
        ]
        for bit in bits[1:]:
            got = swap(jnp.concatenate(parts[1::2], 0), bit)
            size = parts[0].shape[0]
            parts = [
                jnp.concatenate([v, got[i * size : (i + 1) * size]], 0)
                for i, v in enumerate(parts[::2])
            ]
        return parts[0]

    def give_back(values):
        parts = [values]
        for bit in bits[::-1]:
            size = parts[0].shape[0] // 2
            got = swap(jnp.concatenate([v[size:] for v in parts], 0), bit)
            parts = [v[:size] for v in parts] + [
                got[i * size : (i + 1) * size] for i in range(len(parts))
            ]
        index = [0]
        for bit in bits[::-1]:
            index = index + [m | bit for m in index]
        return jnp.concatenate([parts[index.index(m)] for m in range(plane)], 0)

    row_adapter = (jnp.arange(plane * rows) % rows) // capacity
    col_adapter = jnp.arange(depth * block) // rank
    mask = row_adapter[:, None] == col_adapter[None, :]

    def masked(values):
        return jnp.where(mask, values, 0.0).astype(bf16)

    def grad(hid, values, *more):
        out = adapter_scale * dot(hid, values, ((0,), (0,)))
        for m in more:
            out = out + m.astype(f32)
        return out

    def near(u1, d1):
        return jnp.where((z == 0) | (z == 2), d1, u1)

    def middle(u1, d1, e2):
        return jnp.where(edge, e2, jnp.where(z == 1, d1, u1))

    def spread_pair(p):
        return spread.reshape(plane, 2, rows // 2, tok_count)[:, p].reshape(-1, tok_count)

    whole = lax.all_gather(piece, ("chain", "side", "core", "groups"), axis=0, tiled=True)

    turned = [turn(up_rows, k) for k in range(1, depth)]
    cot = dispatch(spread, cotangent)
    spreads = [spread_pair(p) for p in range(2)]

    a = [down_rows[:, :half], down_rows[:, half:]]
    a[1] = tie(a[1], cot)
    one = [(up(v), down(v)) for v in a]
    x0 = dispatch(spreads[0], tokens, cot)
    x1 = dispatch(spreads[1], tokens, x0, *one[0])

    by_shift = jnp.stack([up_rows] + turned)
    up_all = jnp.concatenate(
        [
            lax.dynamic_index_in_dim(by_shift, (z - order[j] + depth) % depth, 0, False)
            for j in range(depth)
        ],
        axis=0,
    )
    hidden = masked(dot(cot, up_all, ((1,), (1,))))

    def pair(p):
        cut = hidden.reshape(plane, 2, rows // 2, depth * block)[:, p]
        return cut.reshape(plane * rows // 2, depth * block)[
            :, p * 2 * block : (p + 1) * 2 * block
        ]

    pairs = [pair(p) for p in range(2)]
    hid = [pairs[j // 2][:, j % 2 * block : (j % 2 + 1) * block] for j in range(depth)]
    second = jnp.where(edge, hid[1], hid[0])

    def lora(p, weights):
        return (adapter_scale * dot(pairs[p], weights, ((1,), (0,)))).astype(bf16)

    def cols(values, h):
        return values[:, h * half : (h + 1) * half]

    two = [None, None]
    for h in range(2):
        v = grad(hid[0], cols(x0, h)).astype(bf16)
        two[h] = (
            up(jnp.where(z == 0, v, one[h][0])),
            down(jnp.where(z == depth - 1, v, one[h][1])),
        )
    near_a = jnp.concatenate([near(*one[h]) for h in range(2)], 1)
    back_1 = give_back(tie(lora(1, jnp.concatenate([near_a, down_rows], 0)), x1))

    three, e2 = [None, None], [None, None]
    for h in range(2):
        uu, dd = two[h]
        e2[h] = jnp.where(z >= 2, uu, dd)
        r1 = jnp.where(edge, jnp.zeros_like(uu), jnp.where(z == 1, uu, dd))
        v = grad(second, cols(x0, h), r1).astype(bf16)
        send_up, send_down = jnp.where(z <= 1, v, e2[h]), jnp.where(z >= 2, v, e2[h])
        if h == 1:
            send_up, send_down = tie(send_up, x1), tie(send_down, x1)
        three[h] = up(send_up), down(send_down)

    four, far_a, back_0 = [None, None], [None, None], [None, None]
    for h in range(2):
        uu, dd = three[h]
        e3 = jnp.where(z == depth - 1, uu, dd)
        zero = jnp.zeros_like(uu)
        ru, rd = jnp.where(edge, zero, uu), jnp.where(edge, zero, dd)
        far_a[h] = jnp.concatenate([jnp.where(edge, e3, e2[h]), middle(*one[h], e2[h])], 0)
        y0, y1 = cols(x0, h), cols(x1, h)
        third_up = grad(hid[2], y1, ru)
        third_down = grad(hid[2], y1, rd)
        inner = grad(hid[1], y0)
        third_up = jnp.where(z == 1, inner + ru.astype(f32), third_up)
        third_down = jnp.where(z == 2, inner + rd.astype(f32), third_down)
        third_up, third_down = third_up.astype(bf16), third_down.astype(bf16)
        if h == 1:
            third_up, third_down = tie(third_up, back_1), tie(third_down, back_1)
        four[h] = up(third_up), down(third_down)
        back_0[h] = give_back(tie(lora(0, far_a[h]), back_1 if h == 0 else back_0[0]))
    far_a = jnp.concatenate(far_a, 1)
    back_0 = jnp.concatenate(back_0, 1)

    down_all = jnp.concatenate([far_a, near_a, down_rows], 0)

    def cut(values, p):
        return values.reshape(plane, 2, rows // 2, -1)[:, p].reshape(plane * rows // 2, -1)

    cots = [cut(cot, p) for p in range(2)]
    masks = [
        cut(mask, p)[:, p * 2 * block : (p + 1) * 2 * block] for p in range(2)
    ]
    shrunk = [
        jnp.where(
            masks[p],
            dot(v, down_all[p * 2 * block : (p + 1) * 2 * block], ((1,), (1,))),
            0.0,
        ).astype(bf16)
        for p, v in enumerate((x0, x1))
    ]
    up_parts = jnp.concatenate(
        [adapter_scale * dot(shrunk[p], cots[p], ((0,), (0,))) for p in range(2)], 0
    )
    up_own = up_parts[(depth - 1) * block :]
    up_parts = up_parts.astype(bf16).reshape(depth, block, features)
    up_sent = [
        turn(lax.dynamic_index_in_dim(up_parts, place[(z + k) % depth], 0, False), k)
        for k in range(1, depth)
    ]
    expanded = jnp.concatenate(
        [
            (
                adapter_scale
                * dot(shrunk[p], up_all[p * 2 * block : (p + 1) * 2 * block], ((1,), (0,)))
            ).astype(bf16)
            for p in range(2)
        ],
        1,
    )
    frozen_out = dot(tokens, whole, ((1,), (0,)))
    frozen_grad = dot(cotangent, whole, ((1,), (1,)))
    expanded = give_back(tie(expanded, back_0, frozen_out, frozen_grad))

    key_output = (
        frozen_out
        + dot(spreads[0], expanded[:, :features], ((0,), (0,)))
        + dot(spreads[1], expanded[:, features:], ((0,), (0,)))
    ).astype(bf16)
    token_grad = (
        frozen_grad
        + dot(spreads[1], back_1, ((0,), (0,)))
        + dot(spreads[0], back_0, ((0,), (0,)))
    ).astype(bf16)
    down_grad = grad(hid[3], x1, *(jnp.concatenate(v, 1) for v in zip(*four)))
    up_grad = up_own + sum(v.astype(f32) for v in up_sent)
    down_grad = jnp.transpose(down_grad.reshape(locals_, rank, width), (0, 2, 1))
    up_grad = up_grad.reshape(locals_, rank, features)
    return key_output, token_grad, down_grad, up_grad


def solution(mesh):
    groups, wide = mesh.devices.shape
    fine = Mesh(
        mesh.devices.reshape(groups, CHAIN, wide // CHAIN // 2, 2),
        ("groups", "chain", "side", "core"),
    )
    every = ("groups", "chain", "side", "core")
    return jax.shard_map(
        shards,
        mesh=fine,
        in_specs=(
            P(every, None),
            P(every, None),
            P(every[1:], None),
            P(every, None, None),
            P(every, None, None),
            P(every, None),
            P("groups"),
        ),
        out_specs=(
            P(every, None),
            P(every, None),
            P(every, None, None),
            P(every, None, None),
        ),
        check_vma=False,
    )
```

```python
import jax
import jax.numpy as jnp
from jax import lax
from jax.sharding import Mesh, PartitionSpec as P

adapter_scale = 0.25
bf16 = jnp.bfloat16
f32 = jnp.float32
CHAIN = 4
ORDER = ((3, 2, 1, 0), (3, 2, 0, 1), (0, 1, 3, 2), (0, 1, 2, 3))
RANK = tuple(tuple(row.index(k) for k in range(CHAIN)) for row in ORDER)


def dot(a, b, dims):
    return lax.dot_general(a, b, (dims, ((), ())), preferred_element_type=f32)


def tie(value, *after):
    odd = False
    for v in after:
        first = v[(0,) * v.ndim]
        odd = odd | (first != first)
    return jnp.where(odd, jnp.zeros_like(value), value)


def shards(
    tokens,
    cotangent,
    frozen_key_matrix,
    adapter_down_weight,
    adapter_up_weight,
    token_adapter_index,
    adapter_storage_index,
):
    groups = lax.axis_size("groups")
    depth = lax.axis_size("chain")
    sides = lax.axis_size("side")
    plane = 2 * sides
    devices = depth * plane
    tok_count = tokens.shape[0]
    locals_, width, rank = adapter_down_weight.shape
    features = cotangent.shape[1]
    entries = adapter_storage_index.shape[0]
    capacity = max(2, 5 * tok_count // (3 * locals_ * devices))
    block = locals_ * rank
    half = width // 2
    used = depth // 2 * locals_ * capacity
    rows = -(-used // 8) * 8
    across = ("side", "core")
    z = lax.axis_index("chain")
    side = lax.axis_index("side")
    q = 2 * side + lax.axis_index("core")
    group = lax.axis_index("groups")
    edge = (z == 0) | (z == depth - 1)
    order = lax.dynamic_index_in_dim(jnp.array(ORDER, jnp.int32), z, 0, False)
    place = lax.dynamic_index_in_dim(jnp.array(RANK, jnp.int32), z, 0, False)

    def turn(values, k):
        return lax.ppermute(values, "chain", [(i, (i + k) % depth) for i in range(depth)])

    def up(values):
        return lax.ppermute(values, "chain", [(i, i + 1) for i in range(depth - 1)])

    def down(values):
        return lax.ppermute(values, "chain", [(i + 1, i) for i in range(depth - 1)])

    down_rows = jnp.transpose(adapter_down_weight, (0, 2, 1)).reshape(block, width)
    up_rows = adapter_up_weight.reshape(block, features)
    share = frozen_key_matrix.shape[0] // groups
    piece = lax.dynamic_slice_in_dim(frozen_key_matrix, group * share, share, 0)
    flat_ids = token_adapter_index[:, 0]
    onehot = (flat_ids[:, None] == jnp.arange(entries, dtype=jnp.int32)[None, :]).astype(jnp.int32)
    within = jnp.sum(jnp.cumsum(onehot, axis=0) * onehot, axis=1) - 1
    position = jnp.sum(onehot * adapter_storage_index[None, :], axis=1)
    home, local = position // locals_, position % locals_
    far = home // plane
    chunk = jnp.sum(
        jnp.where(far[:, None] == jnp.arange(depth, dtype=jnp.int32)[None, :], place[None, :], 0),
        axis=1,
    )
    slots = (home % plane) * rows + (chunk % 2 * locals_ + local) * capacity + within
    numbers = jnp.arange(plane * rows, dtype=jnp.int32)[:, None]
    spreads = [
        ((numbers == slots[None, :]) & (chunk // 2 == p)[None, :]).astype(bf16)
        for p in range(2)
    ]

    def exchange(values):
        return lax.all_to_all(values, across, split_axis=0, concat_axis=0, tiled=True)

    def spread_out(p, values):
        return dot(spreads[p], values, ((1,), (0,))).astype(bf16)

    row_adapter = (jnp.arange(plane * rows) % rows) // capacity
    col_adapter = jnp.arange(2 * block) // rank
    mask = row_adapter[:, None] == col_adapter[None, :]

    def masked(values):
        return jnp.where(mask, values, 0.0).astype(bf16)

    def grad(hid, values, *more):
        out = adapter_scale * dot(hid, values, ((0,), (0,)))
        for m in more:
            out = out + m.astype(f32)
        return out

    def near(u1, d1):
        return jnp.where((z == 0) | (z == 2), d1, u1)

    def middle(u1, d1, e2):
        return jnp.where(edge, e2, jnp.where(z == 1, d1, u1))

    ups = lax.all_gather(up_rows, "chain", axis=0, tiled=False)
    up_all = jnp.concatenate(
        [lax.dynamic_index_in_dim(ups, order[j], 0, False) for j in range(depth)], axis=0
    )
    piece = tie(piece, ups)
    whole = lax.all_gather(piece, ("chain", "side", "core", "groups"), axis=0, tiled=True)

    a = [down_rows[:, :half], down_rows[:, half:]]
    one = [(up(v), down(v)) for v in a]
    cots = exchange(jnp.concatenate([spread_out(p, cotangent) for p in range(2)], 1))
    cots = [cots[:, :features], cots[:, features:]]
    x0 = exchange(spread_out(0, tokens))
    x1 = exchange(tie(spread_out(1, tokens), x0))

    def up_pair(p):
        return up_all[p * 2 * block : (p + 1) * 2 * block]

    pairs = [masked(dot(cots[p], up_pair(p), ((1,), (1,)))) for p in range(2)]
    hid = [pairs[j // 2][:, j % 2 * block : (j % 2 + 1) * block] for j in range(depth)]
    second = jnp.where(edge, hid[1], hid[0])

    def lora(p, weights):
        return (adapter_scale * dot(pairs[p], weights, ((1,), (0,)))).astype(bf16)

    def cols(values, h):
        return values[:, h * half : (h + 1) * half]

    two = [None, None]
    for h in range(2):
        v = grad(hid[0], cols(x0, h)).astype(bf16)
        two[h] = (
            up(jnp.where(z == 0, v, one[h][0])),
            down(jnp.where(z == depth - 1, v, one[h][1])),
        )
    near_a = jnp.concatenate([near(*one[h]) for h in range(2)], 1)
    back_1 = exchange(tie(lora(1, jnp.concatenate([near_a, down_rows], 0)), x1))

    three, e2 = [None, None], [None, None]
    for h in range(2):
        uu, dd = two[h]
        e2[h] = jnp.where(z >= 2, uu, dd)
        r1 = jnp.where(edge, jnp.zeros_like(uu), jnp.where(z == 1, uu, dd))
        v = grad(second, cols(x0, h), r1).astype(bf16)
        send_up, send_down = jnp.where(z <= 1, v, e2[h]), jnp.where(z >= 2, v, e2[h])
        if h == 1:
            send_up, send_down = tie(send_up, x1), tie(send_down, x1)
        three[h] = up(send_up), down(send_down)

    frozen_out = dot(tokens, whole, ((1,), (0,)))
    frozen_grad = dot(cotangent, whole, ((1,), (1,)))
    four, far_a, back_0 = [None, None], [None, None], [None, None]
    for h in range(2):
        uu, dd = three[h]
        e3 = jnp.where(z == depth - 1, uu, dd)
        zero = jnp.zeros_like(uu)
        ru, rd = jnp.where(edge, zero, uu), jnp.where(edge, zero, dd)
        far_a[h] = jnp.concatenate([jnp.where(edge, e3, e2[h]), middle(*one[h], e2[h])], 0)
        y0, y1 = cols(x0, h), cols(x1, h)
        third_up = grad(hid[2], y1, ru)
        third_down = grad(hid[2], y1, rd)
        inner = grad(hid[1], y0)
        third_up = jnp.where(z == 1, inner + ru.astype(f32), third_up)
        third_down = jnp.where(z == 2, inner + rd.astype(f32), third_down)
        third_up, third_down = third_up.astype(bf16), third_down.astype(bf16)
        done = (back_1,) if h == 0 else (frozen_out, frozen_grad)
        third_up, third_down = tie(third_up, *done), tie(third_down, *done)
        four[h] = up(third_up), down(third_down)
        back_0[h] = exchange(tie(lora(0, far_a[h]), back_1 if h == 0 else back_0[0]))
    far_a = jnp.concatenate(far_a, 1)
    back_0 = jnp.concatenate(back_0, 1)

    down_all = jnp.concatenate([far_a, near_a, down_rows], 0)

    shrunk = [
        masked(dot(v, down_all[p * 2 * block : (p + 1) * 2 * block], ((1,), (1,))))
        for p, v in enumerate((x0, x1))
    ]
    up_parts = jnp.concatenate(
        [adapter_scale * dot(shrunk[p], cots[p], ((0,), (0,))) for p in range(2)], 0
    )
    up_own = up_parts[(depth - 1) * block :]
    up_parts = up_parts.astype(bf16).reshape(depth, block, features)
    up_sent = [
        turn(lax.dynamic_index_in_dim(up_parts, place[(z + k) % depth], 0, False), k)
        for k in range(1, depth)
    ]
    expanded = jnp.concatenate(
        [
            (
                adapter_scale
                * dot(shrunk[p], up_pair(p), ((1,), (0,)))
            ).astype(bf16)
            for p in range(2)
        ],
        1,
    )
    expanded = exchange(tie(expanded, back_0))

    key_output = (
        frozen_out
        + dot(spreads[0], expanded[:, :features], ((0,), (0,)))
        + dot(spreads[1], expanded[:, features:], ((0,), (0,)))
    ).astype(bf16)
    token_grad = (
        frozen_grad
        + dot(spreads[1], back_1, ((0,), (0,)))
        + dot(spreads[0], back_0, ((0,), (0,)))
    ).astype(bf16)
    down_grad = grad(hid[3], x1, *(jnp.concatenate(v, 1) for v in zip(*four)))
    up_grad = up_own + sum(v.astype(f32) for v in up_sent)
    down_grad = jnp.transpose(down_grad.reshape(locals_, rank, width), (0, 2, 1))
    up_grad = up_grad.reshape(locals_, rank, features)
    return key_output, token_grad, down_grad, up_grad


def solution(mesh):
    groups, wide = mesh.devices.shape
    fine = Mesh(
        mesh.devices.reshape(groups, CHAIN, wide // CHAIN // 2, 2),
        ("groups", "chain", "side", "core"),
    )
    every = ("groups", "chain", "side", "core")
    return jax.shard_map(
        shards,
        mesh=fine,
        in_specs=(
            P(every, None),
            P(every, None),
            P(every[1:], None),
            P(every, None, None),
            P(every, None, None),
            P(every, None),
            P("groups"),
        ),
        out_specs=(
            P(every, None),
            P(every, None),
            P(every, None, None),
            P(every, None, None),
        ),
        check_vma=False,
    )
```

```python
import jax
import jax.numpy as jnp
from jax import lax
from jax.sharding import Mesh, PartitionSpec as P

adapter_scale = 0.25
bf16 = jnp.bfloat16
f32 = jnp.float32
CHAIN = 4
ORDER = ((3, 2, 1, 0), (3, 2, 0, 1), (0, 1, 3, 2), (0, 1, 2, 3))
RANK = tuple(tuple(row.index(k) for k in range(CHAIN)) for row in ORDER)


def dot(a, b, dims):
    return lax.dot_general(a, b, (dims, ((), ())), preferred_element_type=f32)


def tie(value, *after):
    odd = False
    for v in after:
        first = v[(0,) * v.ndim]
        odd = odd | (first != first)
    return jnp.where(odd, jnp.zeros_like(value), value)


def shards(
    tokens,
    cotangent,
    frozen_key_matrix,
    adapter_down_weight,
    adapter_up_weight,
    token_adapter_index,
    adapter_storage_index,
):
    groups = lax.axis_size("groups")
    depth = lax.axis_size("chain")
    sides = lax.axis_size("side")
    plane = 2 * sides
    devices = depth * plane
    tok_count = tokens.shape[0]
    locals_, width, rank = adapter_down_weight.shape
    features = cotangent.shape[1]
    entries = adapter_storage_index.shape[0]
    capacity = max(2, 5 * tok_count // (3 * locals_ * devices))
    block = locals_ * rank
    half = width // 2
    used = depth // 2 * locals_ * capacity
    rows = -(-used // 8) * 8
    across = ("side", "core")
    z = lax.axis_index("chain")
    side = lax.axis_index("side")
    q = 2 * side + lax.axis_index("core")
    group = lax.axis_index("groups")
    edge = (z == 0) | (z == depth - 1)
    order = lax.dynamic_index_in_dim(jnp.array(ORDER, jnp.int32), z, 0, False)
    place = lax.dynamic_index_in_dim(jnp.array(RANK, jnp.int32), z, 0, False)

    def turn(values, k):
        return lax.ppermute(values, "chain", [(i, (i + k) % depth) for i in range(depth)])

    def up(values):
        return lax.ppermute(values, "chain", [(i, i + 1) for i in range(depth - 1)])

    def down(values):
        return lax.ppermute(values, "chain", [(i + 1, i) for i in range(depth - 1)])

    down_rows = jnp.transpose(adapter_down_weight, (0, 2, 1)).reshape(block, width)
    up_rows = adapter_up_weight.reshape(block, features)
    share = frozen_key_matrix.shape[0] // groups
    piece = lax.dynamic_slice_in_dim(frozen_key_matrix, group * share, share, 0)
    flat_ids = token_adapter_index[:, 0]
    onehot = (flat_ids[:, None] == jnp.arange(entries, dtype=jnp.int32)[None, :]).astype(jnp.int32)
    within = jnp.sum(jnp.cumsum(onehot, axis=0) * onehot, axis=1) - 1
    position = jnp.sum(onehot * adapter_storage_index[None, :], axis=1)
    home, local = position // locals_, position % locals_
    far = home // plane
    chunk = jnp.sum(
        jnp.where(far[:, None] == jnp.arange(depth, dtype=jnp.int32)[None, :], place[None, :], 0),
        axis=1,
    )
    slots = (home % plane) * rows + (chunk % 2 * locals_ + local) * capacity + within
    numbers = jnp.arange(plane * rows, dtype=jnp.int32)[:, None]
    spreads = [
        ((numbers == slots[None, :]) & (chunk // 2 == p)[None, :]).astype(bf16)
        for p in range(2)
    ]

    def exchange(values):
        return lax.all_to_all(values, across, split_axis=0, concat_axis=0, tiled=True)

    def spread_out(p, values):
        return dot(spreads[p], values, ((1,), (0,))).astype(bf16)

    row_adapter = (jnp.arange(plane * rows) % rows) // capacity
    col_adapter = jnp.arange(2 * block) // rank
    mask = row_adapter[:, None] == col_adapter[None, :]

    def masked(values):
        return jnp.where(mask, values, 0.0).astype(bf16)

    def grad(hid, values, *more):
        out = adapter_scale * dot(hid, values, ((0,), (0,)))
        for m in more:
            out = out + m.astype(f32)
        return out

    def near(u1, d1):
        return jnp.where((z == 0) | (z == 2), d1, u1)

    def middle(u1, d1, e2):
        return jnp.where(edge, e2, jnp.where(z == 1, d1, u1))

    ups = lax.all_gather(up_rows, "chain", axis=0, tiled=False)
    up_all = jnp.concatenate(
        [lax.dynamic_index_in_dim(ups, order[j], 0, False) for j in range(depth)], axis=0
    )

    a = [down_rows[:, :half], down_rows[:, half:]]
    one = [(up(v), down(v)) for v in a]
    cots = exchange(jnp.concatenate([spread_out(p, cotangent) for p in range(2)], 1))
    piece = tie(piece, cots)
    whole = lax.all_gather(piece, ("chain", "side", "core", "groups"), axis=0, tiled=True)
    cots = [cots[:, :features], cots[:, features:]]
    x0 = exchange(spread_out(0, tokens))
    x1 = exchange(tie(spread_out(1, tokens), x0))

    def up_pair(p):
        return up_all[p * 2 * block : (p + 1) * 2 * block]

    pairs = [masked(dot(cots[p], up_pair(p), ((1,), (1,)))) for p in range(2)]
    hid = [pairs[j // 2][:, j % 2 * block : (j % 2 + 1) * block] for j in range(depth)]
    second = jnp.where(edge, hid[1], hid[0])

    def lora(p, weights):
        return (adapter_scale * dot(pairs[p], weights, ((1,), (0,)))).astype(bf16)

    def cols(values, h):
        return values[:, h * half : (h + 1) * half]

    two = [None, None]
    for h in range(2):
        v = grad(hid[0], cols(x0, h)).astype(bf16)
        two[h] = (
            up(jnp.where(z == 0, v, one[h][0])),
            down(jnp.where(z == depth - 1, v, one[h][1])),
        )
    near_a = jnp.concatenate([near(*one[h]) for h in range(2)], 1)
    back_1 = exchange(tie(lora(1, jnp.concatenate([near_a, down_rows], 0)), x1))

    three, e2 = [None, None], [None, None]
    for h in range(2):
        uu, dd = two[h]
        e2[h] = jnp.where(z >= 2, uu, dd)
        r1 = jnp.where(edge, jnp.zeros_like(uu), jnp.where(z == 1, uu, dd))
        v = grad(second, cols(x0, h), r1).astype(bf16)
        send_up, send_down = jnp.where(z <= 1, v, e2[h]), jnp.where(z >= 2, v, e2[h])
        send_up, send_down = tie(send_up, x1), tie(send_down, x1)
        three[h] = up(send_up), down(send_down)

    frozen_out = dot(tokens, whole, ((1,), (0,)))
    frozen_grad = dot(cotangent, whole, ((1,), (1,)))
    four, far_a, back_0 = [None, None], [None, None], [None, None]
    for h in range(2):
        uu, dd = three[h]
        e3 = jnp.where(z == depth - 1, uu, dd)
        zero = jnp.zeros_like(uu)
        ru, rd = jnp.where(edge, zero, uu), jnp.where(edge, zero, dd)
        far_a[h] = jnp.concatenate([jnp.where(edge, e3, e2[h]), middle(*one[h], e2[h])], 0)
        y0, y1 = cols(x0, h), cols(x1, h)
        third_up = grad(hid[2], y1, ru)
        third_down = grad(hid[2], y1, rd)
        inner = grad(hid[1], y0)
        third_up = jnp.where(z == 1, inner + ru.astype(f32), third_up)
        third_down = jnp.where(z == 2, inner + rd.astype(f32), third_down)
        third_up, third_down = third_up.astype(bf16), third_down.astype(bf16)
        third_up, third_down = tie(third_up, back_1), tie(third_down, back_1)
        four[h] = up(third_up), down(third_down)
        back_0[h] = exchange(tie(lora(0, far_a[h]), back_1 if h == 0 else back_0[0]))
    far_a = jnp.concatenate(far_a, 1)
    back_0 = jnp.concatenate(back_0, 1)

    down_all = jnp.concatenate([far_a, near_a, down_rows], 0)

    shrunk = [
        masked(dot(v, down_all[p * 2 * block : (p + 1) * 2 * block], ((1,), (1,))))
        for p, v in enumerate((x0, x1))
    ]
    up_parts = jnp.concatenate(
        [adapter_scale * dot(shrunk[p], cots[p], ((0,), (0,))) for p in range(2)], 0
    )
    up_own = up_parts[(depth - 1) * block :]
    up_parts = up_parts.astype(bf16).reshape(depth, block, features)
    up_sent = [
        turn(lax.dynamic_index_in_dim(up_parts, place[(z + k) % depth], 0, False), k)
        for k in range(1, depth)
    ]
    expanded = jnp.concatenate(
        [
            (
                adapter_scale
                * dot(shrunk[p], up_pair(p), ((1,), (0,)))
            ).astype(bf16)
            for p in range(2)
        ],
        1,
    )
    expanded = exchange(tie(expanded, back_0, frozen_out, frozen_grad))

    key_output = (
        frozen_out
        + dot(spreads[0], expanded[:, :features], ((0,), (0,)))
        + dot(spreads[1], expanded[:, features:], ((0,), (0,)))
    ).astype(bf16)
    token_grad = (
        frozen_grad
        + dot(spreads[1], back_1, ((0,), (0,)))
        + dot(spreads[0], back_0, ((0,), (0,)))
    ).astype(bf16)
    down_grad = grad(hid[3], x1, *(jnp.concatenate(v, 1) for v in zip(*four)))
    up_grad = up_own + sum(v.astype(f32) for v in up_sent)
    down_grad = jnp.transpose(down_grad.reshape(locals_, rank, width), (0, 2, 1))
    up_grad = up_grad.reshape(locals_, rank, features)
    return key_output, token_grad, down_grad, up_grad


def solution(mesh):
    groups, wide = mesh.devices.shape
    fine = Mesh(
        mesh.devices.reshape(groups, CHAIN, wide // CHAIN // 2, 2),
        ("groups", "chain", "side", "core"),
    )
    every = ("groups", "chain", "side", "core")
    return jax.shard_map(
        shards,
        mesh=fine,
        in_specs=(
            P(every, None),
            P(every, None),
            P(every[1:], None),
            P(every, None, None),
            P(every, None, None),
            P(every, None),
            P("groups"),
        ),
        out_specs=(
            P(every, None),
            P(every, None),
            P(every, None, None),
            P(every, None, None),
        ),
        check_vma=False,
    )
```
